512 devices in a mesh: seq: 64 (over x, z), tp: 8 (over y, core).
Axes of the slice: x: 4, y: 4, z: 16, core: 2. Of those that a mesh axis runs over, the one named last changes fastest.
Arguments:
- queries: bfloat16 [8192, 4096], P('seq', 'tp'), may hold values from -6 to 6
- block_kv: bfloat16 [8192, 1792], P('seq'), may hold values from -6 to 6
- nb_states: bfloat16 [640, 128, 896], P('seq', 'tp'), may hold values from -6 to 6
- key_weight: bfloat16 [896, 4096], P('seq', 'tp'), may hold values from -1 to 1
- value_weight: bfloat16 [896, 4096], P('seq', 'tp'), may hold values from -0.1875 to 0.1875
- counts: int32 [128], P('seq'), may hold values from 2 to 8, as said below
- owner_slot: int32 [640], P('seq'), may hold values from 0 to 9, as said below
- out_grad: bfloat16 [8192, 4096], P('seq', 'tp'), may hold values from -6 to 6
Outputs:
- attended: bfloat16 [8192, 4096], P('seq', 'tp')
- query_grad: float32 [8192, 4096], P('seq', 'tp')
- key_grad: float32 [896, 4096], P('seq', 'tp')
- value_grad: float32 [896, 4096], P('seq', 'tp')
The draws below stay inside these ranges and needn't reach their ends.
Inputs may be any that keep to these rules, and one draw needn't show every extreme that they name: `counts`: blocks 2k and 2k + 1 have 10 neighbours together, so each device's blocks have 10; a block with 8 occurs in every draw. `owner_slot`: each device's 10 entries (its neighbours in block order) are a permutation of 0 to 9; entry r stores the neighbour r // 2 devices further along seq, cyclically, in row r of that device's block of nb_states.
All inputs are finite; a program needn't handle non-finite values.
Results may differ from the reference program's by a relative error of at most 0.019.
The reference program's roundings to bfloat16 on the way count: a program that leaves them out, or rounds other values in their place, can miss the bound.
Values may be sent and summed in bfloat16 or wider, within the bound.
A program may use at most 64 MiB of HBM per device.

```python
import jax
import jax.numpy as jnp
from jax import lax

HQ = 32
HS = 128
E = 896
NT = 128
CT = 64
BLK_DEV = 2
NB_DEV = 10
CAP = 2
QW = 4096
BLOCKS = 128
TOKENS = 8192
NEIGH = 640
N_SEQ = 64


def shuffle(branch_key):
    return jax.random.permutation(branch_key, NB_DEV)


def draw_counts(key, part):
    key = jax.random.fold_in(key, 11)
    pair_count = BLOCKS // 2
    first_key, second_key = jax.random.split(key)
    first = jax.random.randint(first_key, (pair_count,), 2, 9)
    marked = jax.random.randint(second_key, (), 0, pair_count)
    first = jnp.where(jnp.arange(pair_count) == marked, 8, first)
    return jnp.stack([first, 10 - first], axis=1).reshape(BLOCKS).astype(jnp.int32)


def draw_owner_slot(key, part):
    key = jax.random.fold_in(key, 12)
    device_keys = jax.random.split(key, N_SEQ)
    orders = jax.vmap(shuffle)(device_keys)
    return orders.reshape(NEIGH).astype(jnp.int32)


def draw_queries(key, part):
    key = jax.random.fold_in(key, 21)
    noise_key = jax.random.fold_in(key, 0)
    noise_base = jax.random.truncated_normal(noise_key, -6.0, 6.0, (TOKENS, QW), jnp.float32)
    return noise_base.astype(jnp.bfloat16)


def draw_block_kv(key, part):
    key = jax.random.fold_in(key, 22)
    noise_base = jax.random.truncated_normal(key, -6.0, 6.0, (TOKENS, 2 * E), jnp.float32)
    return noise_base.astype(jnp.bfloat16)


def draw_nb_states(key, part):
    key = jax.random.fold_in(key, 23)
    noise_key = jax.random.fold_in(key, 0)
    noise_base = jax.random.truncated_normal(noise_key, -6.0, 6.0, (NEIGH, NT, E), jnp.float32)
    return noise_base.astype(jnp.bfloat16)


def draw_key_weight(key, part):
    key = jax.random.fold_in(key, 24)
    noise_base = jax.random.truncated_normal(key, -6.0, 6.0, (E, QW), jnp.float32) * E ** (-0.5)
    return noise_base.astype(jnp.bfloat16)


def levels(stream_key, shape, cuts, smallest, high):
    level = 1.0
    for dim, shards_of in cuts:
        steps = jax.random.uniform(jax.random.fold_in(jax.random.fold_in(stream_key, 6), dim), (shards_of,), jnp.float32, smallest / len(cuts), high / len(cuts))
        level = level * jnp.repeat(jnp.exp(steps), shape[dim] // shards_of).reshape((-1,) + (1,) * (len(shape) - 1 - dim))
    return level


def scatter_about(key, extent, width, most, cuts=(), kind=jnp.bfloat16):
    result = width * jax.random.normal(key, extent, jnp.float32)
    if cuts:
        result = result * levels(key, extent, cuts, -0.22, 0.18)
    return jnp.clip(result, -most, most).astype(kind)


def setup_inputs(seed: int = 0) -> dict:
    arg_keys = jax.random.split(jax.random.key(seed), 9)
    queries = draw_queries(jax.random.fold_in(arg_keys[8], 71), 0)
    block_kv = draw_block_kv(jax.random.fold_in(arg_keys[8], 71), 0)
    nb_states = draw_nb_states(jax.random.fold_in(arg_keys[8], 71), 0)
    key_weight = draw_key_weight(jax.random.fold_in(arg_keys[8], 71), 0)
    value_weight = scatter_about(arg_keys[4], (E, QW), E ** -0.5, 0.1875, ((0, 64), (1, 8)))
    counts = draw_counts(jax.random.fold_in(arg_keys[8], 71), 0)
    owner_slot = draw_owner_slot(jax.random.fold_in(arg_keys[8], 71), 0)
    out_grad = scatter_about(arg_keys[7], (TOKENS, QW), 1.0, 6.0, ((0, 64), (1, 8)))
    return {"queries": queries, "block_kv": block_kv, "nb_states": nb_states, "key_weight": key_weight, "value_weight": value_weight, "counts": counts, "owner_slot": owner_slot, "out_grad": out_grad}


def to_half(values):
    return lax.optimization_barrier(values.astype(jnp.bfloat16))


def encode(states, keys_vals, head_size):
    slot_count, row_count, enc_width = states.shape
    head_count = enc_width // head_size
    block_len = keys_vals.shape[1]
    query_heads = states.astype(jnp.float32).reshape(slot_count, row_count, head_count, head_size)
    key_heads = keys_vals[:, :, :enc_width].astype(jnp.float32).reshape(slot_count, block_len, head_count, head_size)
    value_heads = keys_vals[:, :, enc_width:].astype(jnp.float32).reshape(slot_count, block_len, head_count, head_size)
    scores = jnp.einsum("rqhd,rkhd->rhqk", query_heads, key_heads) * (head_size ** -0.5)
    weights = to_half(jax.nn.softmax(scores, axis=-1)).astype(jnp.float32)
    mixed_out = jnp.einsum("rhqk,rkhd->rqhd", weights, value_heads)
    return (states.astype(jnp.float32) + mixed_out.reshape(slot_count, row_count, enc_width)).astype(jnp.bfloat16)


def attend(block_query, key_rows, value_rows, head_size):
    slot_count, block_len, query_width = block_query.shape
    head_count = query_width // head_size
    key_len = key_rows.shape[1]
    query_heads = block_query.astype(jnp.float32).reshape(slot_count, block_len, head_count, head_size)
    key_heads = key_rows.astype(jnp.float32).reshape(slot_count, key_len, head_count, head_size)
    value_heads = value_rows.astype(jnp.float32).reshape(slot_count, key_len, head_count, head_size)
    scores = jnp.einsum("rqhd,rkhd->rhqk", query_heads, key_heads) * (head_size ** -0.5)
    peak_row = lax.stop_gradient(jnp.max(scores, axis=-1))
    weights = jnp.exp(scores - peak_row[..., None])
    row_total = jnp.sum(weights, axis=-1)
    rounded_w = to_half(weights)
    partial_value = jnp.einsum("rhqk,rkhd->rqhd", rounded_w.astype(jnp.float32), value_heads)
    return partial_value, peak_row, row_total, weights, rounded_w


def attend_back(block_query, key_rows, value_rows, weights, rounded_w, push_grad, lift_grad, head_size):
    slot_count, block_len, query_width = block_query.shape
    head_count = query_width // head_size
    key_len = key_rows.shape[1]
    scaling = head_size ** -0.5
    query_heads = block_query.astype(jnp.float32).reshape(slot_count, block_len, head_count, head_size)
    key_heads = key_rows.astype(jnp.float32).reshape(slot_count, key_len, head_count, head_size)
    value_heads = value_rows.astype(jnp.float32).reshape(slot_count, key_len, head_count, head_size)
    push_half = to_half(push_grad).astype(jnp.float32)
    dprob = jnp.einsum("rqhd,rkhd->rhqk", push_half, value_heads) + lift_grad[..., None]
    dscore = to_half(weights * dprob).astype(jnp.float32)
    dquery = jnp.einsum("rhqk,rkhd->rqhd", dscore, key_heads) * scaling
    dkeys = (jnp.einsum("rhqk,rqhd->rkhd", dscore, query_heads) * scaling).astype(jnp.bfloat16)
    dvalues = jnp.einsum("rhqk,rqhd->rkhd", rounded_w.astype(jnp.float32), push_half).astype(jnp.bfloat16)
    return dquery, dkeys, dvalues


def reference(queries, block_kv, nb_states, key_weight, value_weight, counts, owner_slot, out_grad):
    count_rows = counts.reshape(N_SEQ, BLK_DEV)
    owner_rows = owner_slot.reshape(N_SEQ, NB_DEV)
    block_ends = jnp.cumsum(count_rows, axis=1)
    position = jnp.arange(NB_DEV, dtype=jnp.int32)
    block_of = jnp.sum((position[None, :, None] >= block_ends[:, None, :]).astype(jnp.int32), axis=2)
    device = jnp.arange(N_SEQ, dtype=jnp.int32)[:, None]
    global_block = (device * BLK_DEV + block_of).astype(jnp.int32)
    holder = (device + owner_rows // CAP) % N_SEQ
    global_slot = (holder * NB_DEV + owner_rows).astype(jnp.int32)
    slot_block = jnp.zeros((NEIGH,), jnp.int32).at[global_slot.reshape(-1)].set(global_block.reshape(-1))
    query_blocks = queries.reshape(BLOCKS, CT, QW)
    kv_blocks = block_kv.reshape(BLOCKS, CT, 2 * E)
    encoded_all = encode(nb_states, kv_blocks[slot_block], HS)
    key_full = key_weight.astype(jnp.float32)
    value_full = value_weight.astype(jnp.float32)

    def project(encoded):
        flat = encoded.astype(jnp.float32)
        return jnp.dot(flat, key_full).astype(jnp.bfloat16), jnp.dot(flat, value_full).astype(jnp.bfloat16)

    def slot_forward(inputs):
        encoded, block_id = inputs
        key_rows, value_rows = project(encoded)
        block_query = lax.dynamic_index_in_dim(query_blocks, block_id, 0, keepdims=True)
        partial_value, peak_row, row_total, weights, rounded_w = attend(block_query, key_rows[None], value_rows[None], HS)
        return partial_value[0], peak_row[0], row_total[0]

    partial_value, peak_row, row_total = lax.map(slot_forward, (encoded_all, slot_block))
    block_peak = jnp.full((BLOCKS, HQ, CT), -jnp.inf, jnp.float32).at[slot_block].max(peak_row)
    rescale = jnp.exp(peak_row - block_peak[slot_block])
    denominator = jax.ops.segment_sum(rescale * row_total, slot_block, BLOCKS)
    numerator = jax.ops.segment_sum(jnp.transpose(rescale, (0, 2, 1))[..., None] * partial_value, slot_block, BLOCKS)
    mixed_out = numerator / jnp.transpose(denominator, (0, 2, 1))[..., None]
    attended = mixed_out.reshape(TOKENS, QW).astype(jnp.bfloat16)
    grad_blocks = out_grad.reshape(BLOCKS, CT, HQ, HS).astype(jnp.float32)
    delta_row = jnp.sum(grad_blocks * mixed_out, axis=-1)
    factor = rescale / denominator[slot_block]
    lift_grad = -(factor * jnp.transpose(delta_row, (0, 2, 1))[slot_block])

    def slot_backward(running, inputs):
        weight_grad, query_grad = running
        encoded, block_id, factor_row, lift_row = inputs
        key_rows, value_rows = project(encoded)
        block_query = lax.dynamic_index_in_dim(query_blocks, block_id, 0, keepdims=True)
        partial_one, peak_one, total_one, weights, rounded_w = attend(block_query, key_rows[None], value_rows[None], HS)
        block_grad = lax.dynamic_index_in_dim(grad_blocks, block_id, 0, keepdims=True)
        push_grad = jnp.transpose(factor_row, (1, 0))[None, :, :, None] * block_grad
        dquery, dkeys, dvalues = attend_back(block_query, key_rows[None], value_rows[None], weights, rounded_w, push_grad, lift_row[None], HS)
        stacked = jnp.concatenate([dkeys[0].reshape(NT, QW), dvalues[0].reshape(NT, QW)], axis=1).astype(jnp.float32)
        weight_grad = weight_grad + jnp.dot(encoded.astype(jnp.float32).T, stacked)
        query_grad = query_grad.at[block_id].add(dquery[0].reshape(CT, QW))
        return (weight_grad, query_grad), None

    start = (jnp.zeros((E, 2 * QW), jnp.float32), jnp.zeros((BLOCKS, CT, QW), jnp.float32))
    (weight_grad, query_grad), unused = lax.scan(slot_backward, start, (encoded_all, slot_block, factor, lift_grad))
    return (attended, query_grad.reshape(TOKENS, QW), weight_grad[:, :QW], weight_grad[:, QW:])
```

```python
import functools

import jax
import jax.numpy as jnp
import numpy as np
from jax import lax
from jax.experimental import pallas as pl
from jax.experimental.pallas import tpu as pltpu
from jax.sharding import PartitionSpec as P

HS = 128
REACH = 5
PAD = 16
QUAD = 4
MESH = pl.DeviceIdType.MESH
F32 = jnp.float32
BF16 = jnp.bfloat16


def dot(a, b, dims=((1,), (0,))):
    return lax.dot_general(a, b, (dims, ((), ())), preferred_element_type=F32)


class Sems:
    def __init__(self, send, recv):
        self.send, self.recv, self.used = send, recv, 0
        self.copies = []

    def copy(self, src, dst, device):
        i = self.used
        self.used += 1
        c = pltpu.make_async_remote_copy(
            src_ref=src,
            dst_ref=dst,
            send_sem=self.send.at[i],
            recv_sem=self.recv.at[i],
            device_id=device,
            device_id_type=MESH,
        )
        c.start()
        self.copies.append(c)
        return c

    def finish(self):
        for c in self.copies:
            c.wait_send()


def landed(copies):
    for c in copies:
        c.wait_recv()


def kernel(
    sizes,
    q_ref,
    kv_ref,
    nb_ref,
    wk_ref,
    wv_ref,
    counts_ref,
    owner_ref,
    g_ref,
    att_ref,
    dq_ref,
    gk_ref,
    gv_ref,
    nbf,
    xe,
    perm,
    xg,
    wkb,
    wvb,
    padbuf,
    kb,
    vb,
    dkb,
    dvb,
    bias,
    pbuf,
    stats,
    gkb,
    gvb,
    v_slots_x,
    v_sum_x,
    v_slots_near,
    v_sum_near,
    v_slots_stride,
    k_slots_near,
    k_sum_near,
    k_slots_x,
    k_sum_x,
    k_slots_stride,
    send_sem,
    recv_sem,
):
    nx, nz, ny, nc = sizes
    seq_count = nx * nz
    slot_count, tok, enc = nb_ref.shape
    rows_each = wk_ref.shape[0]
    width = wk_ref.shape[1]
    heads = width // HS
    queries = q_ref.shape[0]
    block_len = queries // 2
    padded = seq_count * PAD
    tp_count = ny * nc
    keys = tp_count * slot_count * tok
    scale = HS ** (-0.5)
    seq, tp = lax.axis_index("seq"), lax.axis_index("tp")
    x, z = seq // nz, lax.rem(seq, nz)
    y, core = tp // nc, lax.rem(tp, nc)

    def at_x(i):
        return {"seq": i * nz + z, "tp": tp}

    def at_z(i):
        return {"seq": x * nz + i, "tp": tp}

    def at_y(i):
        return {"seq": seq, "tp": i * nc + core}

    other_core = {"seq": seq, "tp": y * nc + (1 - core)}

    def at_seq(i):
        return {"seq": i, "tp": tp}

    nq, zq, zr = nz // QUAD, z // QUAD, lax.rem(z, QUAD)

    def x_peer(d):
        return at_x(lax.rem(x + d, nx))

    def y_peer(d):
        return at_y(lax.rem(y + d, ny))

    def z_peer(d):
        return at_z(lax.rem(z + d + nz, nz))

    z_near = (1, -1, 2)
    peers = [z_peer(d) for d in (1, -1, 2, -2)]
    peers += [z_peer(QUAD * d) for d in range(1, nq)]
    peers += [x_peer(d) for d in range(1, nx)]
    peers += [y_peer(d) for d in range(1, ny)]
    peers += [other_core]
    for o in range(1, REACH):
        peers.append(at_seq(lax.rem(seq + o, seq_count)))
        peers.append(at_seq(lax.rem(seq + seq_count - o, seq_count)))
    barrier = pltpu.get_barrier_semaphore()
    for peer in peers:
        pl.semaphore_signal(barrier, inc=1, device_id=peer, device_id_type=MESH)

    for source, target in ((wk_ref, wkb), (wv_ref, wvb)):
        padbuf[...] = jnp.zeros_like(padbuf)
        padbuf[0:rows_each, :] = source[...].astype(F32)
        target[zq, zr, x] = padbuf[...].astype(BF16)
    per = slot_count // REACH
    nbf[0:per] = nb_ref[0:per]
    pl.semaphore_wait(barrier, len(peers))

    sems = Sems(send_sem, recv_sem)

    def send(block, devices):
        return [sems.copy(block, block, device) for device in devices]

    stride_devices = [z_peer(QUAD * d) for d in range(1, nq)]
    near_devices = [z_peer(d) for d in z_near]
    x_devices = [x_peer(d) for d in range(1, nx)]
    y_devices = [y_peer(d) for d in range(1, ny)]
    k_stride = send(wkb.at[zq, zr, x], stride_devices)
    v_stride = send(wvb.at[zq, zr, x], stride_devices)
    arriving = {}
    for o in range(1, REACH):
        arriving[o] = sems.copy(
            nb_ref.at[pl.ds(per * o, per)],
            nbf.at[pl.ds(per * o, per)],
            at_seq(lax.rem(seq + seq_count - o, seq_count)),
        )

    first_count = counts_ref[0]
    member = []
    for r in range(slot_count):
        m = jnp.int32(0)
        for i in range(slot_count):
            m = m + jnp.where(owner_ref[i] == r, jnp.where(first_count <= i, 1, 0), 0)
        member.append(m)

    def place():
        col = lax.broadcasted_iota(jnp.int32, (8, padded), 1)
        chunk, e = col // PAD, lax.rem(col, PAD)
        owner = lax.rem(chunk, nx) * nz + chunk // nx
        want = jnp.where(e < rows_each, owner * rows_each + e, -1)[0:1]
        row = lax.broadcasted_iota(jnp.int32, (enc, padded), 0)
        perm[...] = jnp.where(row == want, 1.0, 0.0).astype(BF16)

    def make_bias():
        slot = lax.rem(lax.broadcasted_iota(jnp.int32, (8, keys), 1) // tok, slot_count)
        owned = jnp.zeros((8, keys), jnp.int32)
        for r in range(slot_count):
            owned = jnp.where(slot == r, member[r], owned)
        block = lax.broadcasted_iota(jnp.int32, (queries, keys), 0) // block_len
        bias[...] = jnp.where(block == owned[0:1], 0.0, -jnp.inf)

    def encode(r0, r1):
        n = (r1 - r0) * tok
        states = nbf[r0:r1].reshape(n, enc)
        slot = r0 + lax.broadcasted_iota(jnp.int32, (n, queries), 0) // tok
        owned = jnp.zeros((n, queries), jnp.int32)
        for r in range(r0, r1):
            owned = jnp.where(slot == r, member[r], owned)
        token_block = lax.broadcasted_iota(jnp.int32, (n, queries), 1) // block_len
        ok = token_block == owned
        for h in range(enc // HS):
            cols = slice(h * HS, (h + 1) * HS)
            mine = states[:, cols]
            s = dot(mine, kv_ref[:, cols], ((1,), (1,))) * scale
            s = jnp.where(ok, s, -jnp.inf)
            p = jnp.exp(s - jnp.max(s, axis=1, keepdims=True))
            w = (p / jnp.sum(p, axis=1, keepdims=True)).astype(BF16)
            mixed = dot(w, kv_ref[:, enc + h * HS : enc + (h + 1) * HS])
            xe[r0 * tok : r1 * tok, cols] = (mine.astype(F32) + mixed).astype(BF16)
        spread = dot(xe[r0 * tok : r1 * tok, :], perm[...]).astype(BF16)
        xg[y, core, r0:r1] = spread.reshape(r1 - r0, tok, padded)
        mine = xg.at[y, core, pl.ds(r0, r1 - r0)]
        return send(mine, y_devices)

    def cross(r0, r1):
        block = xg.at[:, core, pl.ds(r0, r1 - r0)]
        return send(block, [other_core])

    place()
    cut0, cut1 = per, 3 * per
    share0 = encode(0, cut0)
    make_bias()
    landed(k_stride)
    k_x = send(wkb.at[:, zr, x], x_devices)
    landed(v_stride)
    v_near = send(wvb.at[:, zr, x], near_devices)
    landed(arriving[o] for o in (1, 2))
    share1 = encode(cut0, cut1)
    landed(k_x)
    k_near = send(wkb.at[:, zr], near_devices)
    landed(v_near)
    v_x = send(wvb.at[:, :, x], x_devices)
    landed(arriving[o] for o in (3, 4))
    share2 = encode(cut1, slot_count)
    landed(share0)
    crossing = cross(0, cut0)
    landed(share1)
    crossing += cross(cut0, cut1)
    landed(share2)
    crossing += cross(cut1, slot_count)
    landed(k_near)
    landed(crossing)

    half_y = ny // 2
    group_rows = keys // 2

    def project(i, weights, target):
        rows = xg[i * half_y : (i + 1) * half_y].reshape(group_rows, padded)
        at = slice(i * group_rows, (i + 1) * group_rows)
        target[at, :] = dot(rows, weights[...].reshape(padded, width)).astype(BF16)

    for i in range(2):
        project(i, wkb, kb)
    landed(v_x)
    for i in range(2):
        project(i, wvb, vb)

    for h in range(heads):
        cols = slice(h * HS, (h + 1) * HS)
        s = dot(q_ref[:, cols], kb[:, cols], ((1,), (1,))) * scale + bias[...]
        p = jnp.exp(s - jnp.max(s, axis=1, keepdims=True))
        inverse = 1.0 / jnp.sum(p, axis=1, keepdims=True)
        out = dot(p.astype(BF16), vb[:, cols]) * inverse
        att_ref[:, cols] = out.astype(BF16)
        grad = g_ref[:, cols]
        delta = jnp.sum(grad.astype(F32) * out, axis=1, keepdims=True)
        stats[h] = jnp.broadcast_to(delta, (queries, HS))
        p = p * inverse
        pbuf[h] = p
        dvb[:, cols] = dot(p.astype(BF16), grad, ((0,), (0,))).astype(BF16)

    row_tile = padded // nq

    def weight_grad(target, source):
        for i in range(nq):
            lhs = xg[:, :, :, :, i * row_tile : (i + 1) * row_tile].reshape(keys, row_tile)
            part = dot(lhs, source[...], ((0,), (0,)))
            target[i] = part.astype(BF16).reshape(QUAD, nx, PAD, width)

    def exchange_x(block, slots):
        return [
            sems.copy(block(lax.rem(x + d, nx)), slots.at[d - 1], x_peer(d)) for d in range(1, nx)
        ]

    def exchange_near(block, slots):
        half = nq // 2
        copies = []
        for d in (1, -1):
            dst = slots.at[0 if d == 1 else 1]
            copies.append(sems.copy(block(lax.rem(zr + d + QUAD, QUAD)), dst, z_peer(d)))
        for d, first in ((2, 0), (-2, half)):
            src = block(lax.rem(zr + 2, QUAD)).at[pl.ds(first, half)]
            copies.append(sems.copy(src, slots.at[2, pl.ds(first, half)], z_peer(d)))
        return copies

    def exchange_stride(block, slots):
        return [
            sems.copy(block(lax.rem(zq + d, nq)), slots.at[d - 1], z_peer(QUAD * d))
            for d in range(1, nq)
        ]

    def total(own, slots):
        result = own.astype(F32)
        for i in range(slots.shape[0]):
            result = result + slots[i].astype(F32)
        return result

    weight_grad(gvb, dvb)
    gv_x = exchange_x(lambda i: gvb.at[:, :, i], v_slots_x)

    for h in range(heads):
        cols = slice(h * HS, (h + 1) * HS)
        dp = dot(g_ref[:, cols], vb[:, cols], ((1,), (1,)))
        ds = (pbuf[h] * (dp - stats[h][:, 0:1])).astype(BF16)
        dq_ref[:, cols] = dot(ds, kb[:, cols]) * scale
        dkb[:, cols] = (dot(ds, q_ref[:, cols], ((0,), (0,))) * scale).astype(BF16)
    weight_grad(gkb, dkb)
    gk_near = exchange_near(lambda i: gkb.at[:, i], k_slots_near)
    landed(gv_x)
    v_sum_x[...] = total(gvb[:, :, x], v_slots_x).astype(BF16)
    gv_near = exchange_near(lambda i: v_sum_x.at[:, i], v_slots_near)
    landed(gk_near)
    k_sum_near[...] = total(gkb[:, zr], k_slots_near).astype(BF16)
    gk_x = exchange_x(lambda i: k_sum_near.at[:, i], k_slots_x)
    landed(gv_near)
    v_sum_near[...] = total(v_sum_x[:, zr], v_slots_near).astype(BF16)
    gv_stride = exchange_stride(lambda i: v_sum_near.at[i], v_slots_stride)
    landed(gk_x)
    k_sum_x[...] = total(k_sum_near[:, x], k_slots_x).astype(BF16)
    gk_stride = exchange_stride(lambda i: k_sum_x.at[i], k_slots_stride)
    landed(gv_stride)
    gv_ref[...] = total(v_sum_near[zq], v_slots_stride)[0:rows_each]
    landed(gk_stride)
    gk_ref[...] = total(k_sum_x[zq], k_slots_stride)[0:rows_each]
    sems.finish()


def per_device(sizes, queries, block_kv, nb_states, key_weight, value_weight, counts, owner, grad):
    nx, nz, ny, nc = sizes
    tokens, width = queries.shape
    slot_count, tok, enc = nb_states.shape
    rows_each = key_weight.shape[0]
    heads = width // HS
    padded = nx * nz * PAD
    tp_count = ny * nc
    keys = tp_count * slot_count * tok
    nq = nz // QUAD
    copies = 4 * (nx - 1) + 4 * (nq - 1) + 6 + 8 + REACH - 1 + 3 * ny
    vmem = pl.BlockSpec(memory_space=pltpu.VMEM)
    smem = pl.BlockSpec(memory_space=pltpu.SMEM)
    scratch = [
        pltpu.VMEM((slot_count, tok, enc), BF16),
        pltpu.VMEM((slot_count * tok, enc), BF16),
        pltpu.VMEM((enc, padded), BF16),
        pltpu.VMEM((ny, nc, slot_count, tok, padded), BF16),
        pltpu.VMEM((nq, QUAD, nx, PAD, width), BF16),
        pltpu.VMEM((nq, QUAD, nx, PAD, width), BF16),
        pltpu.VMEM((PAD, width), F32),
        pltpu.VMEM((keys, width), BF16),
        pltpu.VMEM((keys, width), BF16),
        pltpu.VMEM((keys, width), BF16),
        pltpu.VMEM((keys, width), BF16),
        pltpu.VMEM((tokens, keys), F32),
        pltpu.VMEM((heads, tokens, keys), F32),
        pltpu.VMEM((heads, tokens, HS), F32),
        pltpu.VMEM((nq, QUAD, nx, PAD, width), BF16),
        pltpu.VMEM((nq, QUAD, nx, PAD, width), BF16),
        pltpu.VMEM((nx - 1, nq, QUAD, PAD, width), BF16),
        pltpu.VMEM((nq, QUAD, PAD, width), BF16),
        pltpu.VMEM((3, nq, PAD, width), BF16),
        pltpu.VMEM((nq, PAD, width), BF16),
        pltpu.VMEM((nq - 1, PAD, width), BF16),
        pltpu.VMEM((3, nq, nx, PAD, width), BF16),
        pltpu.VMEM((nq, nx, PAD, width), BF16),
        pltpu.VMEM((nx - 1, nq, PAD, width), BF16),
        pltpu.VMEM((nq, PAD, width), BF16),
        pltpu.VMEM((nq - 1, PAD, width), BF16),
        pltpu.SemaphoreType.DMA((copies,)),
        pltpu.SemaphoreType.DMA((copies,)),
    ]
    return pl.pallas_call(
        functools.partial(kernel, sizes),
        out_shape=(
            jax.ShapeDtypeStruct((tokens, width), BF16),
            jax.ShapeDtypeStruct((tokens, width), F32),
            jax.ShapeDtypeStruct((rows_each, width), F32),
            jax.ShapeDtypeStruct((rows_each, width), F32),
        ),
        in_specs=[vmem, vmem, vmem, vmem, vmem, smem, smem, vmem],
        out_specs=(vmem, vmem, vmem, vmem),
        scratch_shapes=scratch,
        compiler_params=pltpu.CompilerParams(
            collective_id=0, has_side_effects=True, vmem_limit_bytes=56 * 1024 * 1024
        ),
        cost_estimate=pl.CostEstimate(
            flops=8 * 10**9, bytes_accessed=2 * 10**6, transcendentals=10**6
        ),
    )(queries, block_kv, nb_states, key_weight, value_weight, counts, owner, grad)


def solution(mesh, sizes=(4, 16, 4, 2)):
    in_specs = (
        P("seq", "tp"),
        P("seq", None),
        P("seq", "tp", None),
        P("seq", "tp"),
        P("seq", "tp"),
        P("seq"),
        P("seq"),
        P("seq", "tp"),
    )
    out_specs = (P("seq", "tp"), P("seq", "tp"), P("seq", "tp"), P("seq", "tp"))
    return jax.shard_map(
        functools.partial(per_device, sizes),
        mesh=mesh,
        in_specs=in_specs,
        out_specs=out_specs,
        check_vma=False,
    )
```

```python
import functools

import jax
import jax.numpy as jnp
import numpy as np
from jax import lax
from jax.experimental import pallas as pl
from jax.experimental.pallas import tpu as pltpu
from jax.sharding import PartitionSpec as P

HS = 128
REACH = 5
PAD = 16
QUAD = 4
MESH = pl.DeviceIdType.MESH
F32 = jnp.float32
BF16 = jnp.bfloat16


def dot(a, b, dims=((1,), (0,))):
    return lax.dot_general(a, b, (dims, ((), ())), preferred_element_type=F32)


class Sems:
    def __init__(self, send, recv):
        self.send, self.recv, self.used = send, recv, 0
        self.copies = []

    def copy(self, src, dst, device):
        i = self.used
        self.used += 1
        c = pltpu.make_async_remote_copy(
            src_ref=src,
            dst_ref=dst,
            send_sem=self.send.at[i],
            recv_sem=self.recv.at[i],
            device_id=device,
            device_id_type=MESH,
        )
        c.start()
        self.copies.append(c)
        return c

    def finish(self):
        for c in self.copies:
            c.wait_send()


def landed(copies):
    for c in copies:
        c.wait_recv()


def kernel(
    sizes,
    q_ref,
    kv_ref,
    nb_ref,
    wk_ref,
    wv_ref,
    counts_ref,
    owner_ref,
    g_ref,
    att_ref,
    dq_ref,
    gk_ref,
    gv_ref,
    nbf,
    xe,
    perm,
    xg,
    wkb,
    wvb,
    padbuf,
    kb,
    vb,
    dkb,
    dvb,
    bias,
    pbuf,
    stats,
    gkb,
    gvb,
    v_slots_x,
    v_sum_x,
    v_slots_near,
    v_sum_near,
    v_slots_stride,
    k_slots_near,
    k_sum_near,
    k_slots_x,
    k_sum_x,
    k_slots_stride,
    send_sem,
    recv_sem,
):
    nx, nz, ny, nc = sizes
    seq_count = nx * nz
    slot_count, tok, enc = nb_ref.shape
    rows_each = wk_ref.shape[0]
    width = wk_ref.shape[1]
    heads = width // HS
    queries = q_ref.shape[0]
    block_len = queries // 2
    padded = seq_count * PAD
    tp_count = ny * nc
    keys = tp_count * slot_count * tok
    scale = HS ** (-0.5)
    seq, tp = lax.axis_index("seq"), lax.axis_index("tp")
    x, z = seq // nz, lax.rem(seq, nz)
    y, core = tp // nc, lax.rem(tp, nc)

    def at_x(i):
        return {"seq": i * nz + z, "tp": tp}

    def at_z(i):
        return {"seq": x * nz + i, "tp": tp}

    def at_y(i):
        return {"seq": seq, "tp": i * nc + core}

    other_core = {"seq": seq, "tp": y * nc + (1 - core)}

    def at_seq(i):
        return {"seq": i, "tp": tp}

    nq, zq, zr = nz // QUAD, z // QUAD, lax.rem(z, QUAD)

    def x_peer(d):
        return at_x(lax.rem(x + d, nx))

    def y_peer(d):
        return at_y(lax.rem(y + d, ny))

    def z_peer(d):
        return at_z(lax.rem(z + d + nz, nz))

    z_near = (1, -1, 2)
    peers = [z_peer(d) for d in (1, -1, 2, -2)]
    peers += [z_peer(QUAD * d) for d in range(1, nq)]
    peers += [x_peer(d) for d in range(1, nx)]
    peers += [y_peer(d) for d in range(1, ny)]
    peers += [other_core]
    for o in range(1, REACH):
        peers.append(at_seq(lax.rem(seq + o, seq_count)))
        peers.append(at_seq(lax.rem(seq + seq_count - o, seq_count)))
    barrier = pltpu.get_barrier_semaphore()
    for peer in peers:
        pl.semaphore_signal(barrier, inc=1, device_id=peer, device_id_type=MESH)

    for source, target in ((wk_ref, wkb), (wv_ref, wvb)):
        padbuf[...] = jnp.zeros_like(padbuf)
        padbuf[0:rows_each, :] = source[...].astype(F32)
        target[zq, zr, x] = padbuf[...].astype(BF16)
    per = slot_count // REACH
    nbf[0:per] = nb_ref[0:per]
    pl.semaphore_wait(barrier, len(peers))

    sems = Sems(send_sem, recv_sem)

    def send(block, devices):
        return [sems.copy(block, block, device) for device in devices]

    stride_devices = [z_peer(QUAD * d) for d in range(1, nq)]
    near_devices = [z_peer(d) for d in z_near]
    x_devices = [x_peer(d) for d in range(1, nx)]
    y_devices = [y_peer(d) for d in range(1, ny)]
    k_stride = send(wkb.at[zq, zr, x], stride_devices)
    v_stride = send(wvb.at[zq, zr, x], stride_devices)
    arriving = {}
    for o in range(1, REACH):
        arriving[o] = sems.copy(
            nb_ref.at[pl.ds(per * o, per)],
            nbf.at[pl.ds(per * o, per)],
            at_seq(lax.rem(seq + seq_count - o, seq_count)),
        )

    first_count = counts_ref[0]
    member = []
    for r in range(slot_count):
        m = jnp.int32(0)
        for i in range(slot_count):
            m = m + jnp.where(owner_ref[i] == r, jnp.where(first_count <= i, 1, 0), 0)
        member.append(m)

    def place():
        col = lax.broadcasted_iota(jnp.int32, (8, padded), 1)
        chunk, e = col // PAD, lax.rem(col, PAD)
        owner = lax.rem(chunk, nx) * nz + chunk // nx
        want = jnp.where(e < rows_each, owner * rows_each + e, -1)[0:1]
        row = lax.broadcasted_iota(jnp.int32, (enc, padded), 0)
        perm[...] = jnp.where(row == want, 1.0, 0.0).astype(BF16)

    def make_bias():
        slot = lax.rem(lax.broadcasted_iota(jnp.int32, (8, keys), 1) // tok, slot_count)
        owned = jnp.zeros((8, keys), jnp.int32)
        for r in range(slot_count):
            owned = jnp.where(slot == r, member[r], owned)
        block = lax.broadcasted_iota(jnp.int32, (queries, keys), 0) // block_len
        bias[...] = jnp.where(block == owned[0:1], 0.0, -jnp.inf)

    def encode(r0, r1):
        n = (r1 - r0) * tok
        states = nbf[r0:r1].reshape(n, enc)
        slot = r0 + lax.broadcasted_iota(jnp.int32, (n, queries), 0) // tok
        owned = jnp.zeros((n, queries), jnp.int32)
        for r in range(r0, r1):
            owned = jnp.where(slot == r, member[r], owned)
        token_block = lax.broadcasted_iota(jnp.int32, (n, queries), 1) // block_len
        ok = token_block == owned
        rows = slice(r0 * tok, r1 * tok)
        parts = [slice(h * HS, (h + 1) * HS) for h in range(enc // HS)]
        scores = [dot(states[:, c], kv_ref[:, c], ((1,), (1,))) for c in parts]
        scores = [jnp.where(ok, s * scale, -jnp.inf) for s in scores]
        tops = [jnp.max(s, axis=1, keepdims=True) for s in scores]
        scores = [jnp.exp(s - t) for s, t in zip(scores, tops)]
        sums = [jnp.sum(p, axis=1, keepdims=True) for p in scores]
        scores = [(p / t).astype(BF16) for p, t in zip(scores, sums)]
        mixed = [
            dot(w, kv_ref[:, enc + h * HS : enc + (h + 1) * HS]) for h, w in enumerate(scores)
        ]
        for c, m in zip(parts, mixed):
            xe[rows, c] = (states[:, c].astype(F32) + m).astype(BF16)
        spread = dot(xe[r0 * tok : r1 * tok, :], perm[...]).astype(BF16)
        xg[y, core, r0:r1] = spread.reshape(r1 - r0, tok, padded)
        mine = xg.at[y, core, pl.ds(r0, r1 - r0)]
        return send(mine, y_devices)

    def cross(r0, r1):
        block = xg.at[:, core, pl.ds(r0, r1 - r0)]
        return send(block, [other_core])

    place()
    cut0, cut1 = per, 3 * per
    share0 = encode(0, cut0)
    make_bias()
    landed(k_stride)
    low, high = pl.ds(0, width // 2), pl.ds(width // 2, width // 2)
    k_near = send(wkb.at[:, zr, x, :, low], near_devices)
    l_x = send(wkb.at[:, zr, x, :, high], x_devices)
    k_x = send(wkb.at[:, zr, x, :, low], x_devices)
    l_near = send(wkb.at[:, zr, x, :, high], near_devices)
    landed(v_stride)
    v_near = send(wvb.at[:, zr, x], near_devices)
    v_x = send(wvb.at[:, zr, x], x_devices)
    landed(arriving[o] for o in (1, 2))
    share1 = encode(cut0, cut1)
    for i, d in enumerate(z_near):
        landed(k_near[i : i + 1])
        k_x += send(wkb.at[:, lax.rem(zr + QUAD - d, QUAD), x, :, low], x_devices)
    for d in range(1, nx):
        landed(l_x[d - 1 : d])
        l_near += send(wkb.at[:, zr, lax.rem(x + nx - d, nx), :, high], near_devices)
    for i, d in enumerate(z_near):
        landed(v_near[i : i + 1])
        v_x += send(wvb.at[:, lax.rem(zr + QUAD - d, QUAD), x], x_devices)
    landed(arriving[o] for o in (3, 4))
    share2 = encode(cut1, slot_count)
    landed(share0)
    crossing = cross(0, cut0)
    landed(share1)
    crossing += cross(cut0, cut1)
    landed(share2)
    crossing += cross(cut1, slot_count)
    landed(k_x)
    landed(l_near)
    landed(crossing)

    half_y = ny // 2
    group_rows = keys // 2

    def project(i, weights, target):
        rows = xg[i * half_y : (i + 1) * half_y].reshape(group_rows, padded)
        at = slice(i * group_rows, (i + 1) * group_rows)
        target[at, :] = dot(rows, weights[...].reshape(padded, width)).astype(BF16)

    for i in range(2):
        project(i, wkb, kb)
    landed(v_x)
    for i in range(2):
        project(i, wvb, vb)

    parts = [slice(h * HS, (h + 1) * HS) for h in range(heads)]
    scores = [dot(q_ref[:, c], kb[:, c], ((1,), (1,))) for c in parts]
    scores = [s * scale + bias[...] for s in scores]
    tops = [jnp.max(s, axis=1, keepdims=True) for s in scores]
    weights = [jnp.exp(s - t) for s, t in zip(scores, tops)]
    inverse = [1.0 / jnp.sum(p, axis=1, keepdims=True) for p in weights]
    outs = [dot(p.astype(BF16), vb[:, c]) * t for p, c, t in zip(weights, parts, inverse)]
    weights = [p * t for p, t in zip(weights, inverse)]
    for h, c in enumerate(parts):
        pbuf[h] = weights[h]
        dvb[:, c] = dot(weights[h].astype(BF16), g_ref[:, c], ((0,), (0,))).astype(BF16)
    for h, c in enumerate(parts):
        att_ref[:, c] = outs[h].astype(BF16)
        delta = jnp.sum(g_ref[:, c].astype(F32) * outs[h], axis=1, keepdims=True)
        stats[h] = jnp.broadcast_to(delta, (queries, HS))

    row_tile = padded // nq

    def weight_grad(target, source):
        for i in range(nq):
            lhs = xg[:, :, :, :, i * row_tile : (i + 1) * row_tile].reshape(keys, row_tile)
            part = dot(lhs, source[...], ((0,), (0,)))
            target[i] = part.astype(BF16).reshape(QUAD, nx, PAD, width)

    def exchange_x(block, slots):
        return [
            sems.copy(block(lax.rem(x + d, nx)), slots.at[d - 1], x_peer(d)) for d in range(1, nx)
        ]

    def exchange_near(block, slots):
        half = nq // 2
        copies = []
        for d in (1, -1):
            dst = slots.at[0 if d == 1 else 1]
            copies.append(sems.copy(block(lax.rem(zr + d + QUAD, QUAD)), dst, z_peer(d)))
        for d, first in ((2, 0), (-2, half)):
            src = block(lax.rem(zr + 2, QUAD)).at[pl.ds(first, half)]
            copies.append(sems.copy(src, slots.at[2, pl.ds(first, half)], z_peer(d)))
        return copies

    def exchange_stride(block, slots):
        return [
            sems.copy(block(lax.rem(zq + d, nq)), slots.at[d - 1], z_peer(QUAD * d))
            for d in range(1, nq)
        ]

    def total(own, slots):
        result = own.astype(F32)
        for i in range(slots.shape[0]):
            result = result + slots[i].astype(F32)
        return result

    weight_grad(gvb, dvb)
    gv_x = exchange_x(lambda i: gvb.at[:, :, i], v_slots_x)

    dps = [dot(g_ref[:, c], vb[:, c], ((1,), (1,))) for c in parts]
    dss = [(pbuf[h] * (dp - stats[h][:, 0:1])).astype(BF16) for h, dp in enumerate(dps)]
    for ds, c in zip(dss, parts):
        dkb[:, c] = (dot(ds, q_ref[:, c], ((0,), (0,))) * scale).astype(BF16)
    weight_grad(gkb, dkb)
    gk_near = []
    for d in range(1, nx + 1):
        to = lax.rem(x + d, nx)
        gk_near.append(
            exchange_near(lambda i, to=to: gkb.at[:, i, to], k_slots_near.at[:, :, to])
        )
    for ds, c in zip(dss, parts):
        dq_ref[:, c] = dot(ds, kb[:, c]) * scale
    landed(gv_x)
    v_sum_x[...] = total(gvb[:, :, x], v_slots_x).astype(BF16)
    gv_near = exchange_near(lambda i: v_sum_x.at[:, i], v_slots_near)
    gk_x = []
    for d in range(1, nx + 1):
        to = lax.rem(x + d, nx)
        landed(gk_near[d - 1])
        k_sum_near[:, to] = total(gkb[:, zr, to], k_slots_near.at[:, :, to]).astype(BF16)
        if d < nx:
            gk_x.append(sems.copy(k_sum_near.at[:, to], k_slots_x.at[d - 1], x_peer(d)))
    landed(gv_near)
    v_sum_near[...] = total(v_sum_x[:, zr], v_slots_near).astype(BF16)
    gv_stride = exchange_stride(lambda i: v_sum_near.at[i], v_slots_stride)
    landed(gk_x)
    k_sum_x[...] = total(k_sum_near[:, x], k_slots_x).astype(BF16)
    gk_stride = exchange_stride(lambda i: k_sum_x.at[i], k_slots_stride)
    landed(gv_stride)
    gv_ref[...] = total(v_sum_near[zq], v_slots_stride)[0:rows_each]
    landed(gk_stride)
    gk_ref[...] = total(k_sum_x[zq], k_slots_stride)[0:rows_each]
    sems.finish()


def per_device(sizes, queries, block_kv, nb_states, key_weight, value_weight, counts, owner, grad):
    nx, nz, ny, nc = sizes
    tokens, width = queries.shape
    slot_count, tok, enc = nb_states.shape
    rows_each = key_weight.shape[0]
    heads = width // HS
    padded = nx * nz * PAD
    tp_count = ny * nc
    keys = tp_count * slot_count * tok
    nq = nz // QUAD
    copies = 4 * (nq - 1) + 4 * (nx - 1) + 2 * 3 * nx + (nx - 1) * 3 + 4 * nx + 4
    copies += REACH - 1 + 3 * ny + 4 * (nx - 1) + 3 * nx
    vmem = pl.BlockSpec(memory_space=pltpu.VMEM)
    smem = pl.BlockSpec(memory_space=pltpu.SMEM)
    scratch = [
        pltpu.VMEM((slot_count, tok, enc), BF16),
        pltpu.VMEM((slot_count * tok, enc), BF16),
        pltpu.VMEM((enc, padded), BF16),
        pltpu.VMEM((ny, nc, slot_count, tok, padded), BF16),
        pltpu.VMEM((nq, QUAD, nx, PAD, width), BF16),
        pltpu.VMEM((nq, QUAD, nx, PAD, width), BF16),
        pltpu.VMEM((PAD, width), F32),
        pltpu.VMEM((keys, width), BF16),
        pltpu.VMEM((keys, width), BF16),
        pltpu.VMEM((keys, width), BF16),
        pltpu.VMEM((keys, width), BF16),
        pltpu.VMEM((tokens, keys), F32),
        pltpu.VMEM((heads, tokens, keys), F32),
        pltpu.VMEM((heads, tokens, HS), F32),
        pltpu.VMEM((nq, QUAD, nx, PAD, width), BF16),
        pltpu.VMEM((nq, QUAD, nx, PAD, width), BF16),
        pltpu.VMEM((nx - 1, nq, QUAD, PAD, width), BF16),
        pltpu.VMEM((nq, QUAD, PAD, width), BF16),
        pltpu.VMEM((3, nq, PAD, width), BF16),
        pltpu.VMEM((nq, PAD, width), BF16),
        pltpu.VMEM((nq - 1, PAD, width), BF16),
        pltpu.VMEM((3, nq, nx, PAD, width), BF16),
        pltpu.VMEM((nq, nx, PAD, width), BF16),
        pltpu.VMEM((nx - 1, nq, PAD, width), BF16),
        pltpu.VMEM((nq, PAD, width), BF16),
        pltpu.VMEM((nq - 1, PAD, width), BF16),
        pltpu.SemaphoreType.DMA((copies,)),
        pltpu.SemaphoreType.DMA((copies,)),
    ]
    return pl.pallas_call(
        functools.partial(kernel, sizes),
        out_shape=(
            jax.ShapeDtypeStruct((tokens, width), BF16),
            jax.ShapeDtypeStruct((tokens, width), F32),
            jax.ShapeDtypeStruct((rows_each, width), F32),
            jax.ShapeDtypeStruct((rows_each, width), F32),
        ),
        in_specs=[vmem, vmem, vmem, vmem, vmem, smem, smem, vmem],
        out_specs=(vmem, vmem, vmem, vmem),
        scratch_shapes=scratch,
        compiler_params=pltpu.CompilerParams(
            collective_id=0, has_side_effects=True, vmem_limit_bytes=56 * 1024 * 1024
        ),
        cost_estimate=pl.CostEstimate(
            flops=8 * 10**9, bytes_accessed=2 * 10**6, transcendentals=10**6
        ),
    )(queries, block_kv, nb_states, key_weight, value_weight, counts, owner, grad)


def solution(mesh, sizes=(4, 16, 4, 2)):
    in_specs = (
        P("seq", "tp"),
        P("seq", None),
        P("seq", "tp", None),
        P("seq", "tp"),
        P("seq", "tp"),
        P("seq"),
        P("seq"),
        P("seq", "tp"),
    )
    out_specs = (P("seq", "tp"), P("seq", "tp"), P("seq", "tp"), P("seq", "tp"))
    return jax.shard_map(
        functools.partial(per_device, sizes),
        mesh=mesh,
        in_specs=in_specs,
        out_specs=out_specs,
        check_vma=False,
    )
```

```python
import functools

import jax
import jax.numpy as jnp
import numpy as np
from jax import lax
from jax.experimental import pallas as pl
from jax.experimental.pallas import tpu as pltpu
from jax.sharding import PartitionSpec as P

HS = 128
REACH = 5
PAD = 16
QUAD = 4
MESH = pl.DeviceIdType.MESH
F32 = jnp.float32
BF16 = jnp.bfloat16


def dot(a, b, dims=((1,), (0,))):
    return lax.dot_general(a, b, (dims, ((), ())), preferred_element_type=F32)


class Sems:
    def __init__(self, send, recv):
        self.send, self.recv, self.used = send, recv, 0
        self.copies = []

    def copy(self, src, dst, device):
        i = self.used
        self.used += 1
        c = pltpu.make_async_remote_copy(
            src_ref=src,
            dst_ref=dst,
            send_sem=self.send.at[i],
            recv_sem=self.recv.at[i],
            device_id=device,
            device_id_type=MESH,
        )
        c.start()
        self.copies.append(c)
        return c

    def finish(self):
        for c in self.copies:
            c.wait_send()


def landed(copies):
    for c in copies:
        c.wait_recv()


def kernel(
    sizes,
    q_ref,
    kv_ref,
    nb_ref,
    wk_ref,
    wv_ref,
    counts_ref,
    owner_ref,
    g_ref,
    att_ref,
    dq_ref,
    gk_ref,
    gv_ref,
    nbf,
    xe,
    perm,
    xg,
    wkb,
    wvb,
    padbuf,
    kb,
    vb,
    dkb,
    dvb,
    bias,
    pbuf,
    stats,
    gkb,
    gvb,
    v_slots_x,
    v_sum_x,
    v_slots_near,
    v_sum_near,
    v_slots_stride,
    k_slots_near,
    k_sum_near,
    k_slots_x,
    k_sum_x,
    k_slots_stride,
    send_sem,
    recv_sem,
):
    nx, nz, ny, nc = sizes
    seq_count = nx * nz
    slot_count, tok, enc = nb_ref.shape
    rows_each = wk_ref.shape[0]
    width = wk_ref.shape[1]
    heads = width // HS
    queries = q_ref.shape[0]
    block_len = queries // 2
    padded = seq_count * PAD
    tp_count = ny * nc
    keys = tp_count * slot_count * tok
    scale = HS ** (-0.5)
    seq, tp = lax.axis_index("seq"), lax.axis_index("tp")
    x, z = seq // nz, lax.rem(seq, nz)
    y, core = tp // nc, lax.rem(tp, nc)

    def at_x(i):
        return {"seq": i * nz + z, "tp": tp}

    def at_z(i):
        return {"seq": x * nz + i, "tp": tp}

    def at_y(i):
        return {"seq": seq, "tp": i * nc + core}

    other_core = {"seq": seq, "tp": y * nc + (1 - core)}

    def at_seq(i):
        return {"seq": i, "tp": tp}

    nq, zq, zr = nz // QUAD, z // QUAD, lax.rem(z, QUAD)

    def x_peer(d):
        return at_x(lax.rem(x + d, nx))

    def y_peer(d):
        return at_y(lax.rem(y + d, ny))

    def z_peer(d):
        return at_z(lax.rem(z + d + nz, nz))

    z_near = (1, -1, 2)
    peers = [z_peer(d) for d in (1, -1, 2, -2)]
    peers += [z_peer(QUAD * d) for d in range(1, nq)]
    peers += [x_peer(d) for d in range(1, nx)]
    peers += [y_peer(d) for d in range(1, ny)]
    peers += [other_core]
    for o in range(1, REACH):
        peers.append(at_seq(lax.rem(seq + o, seq_count)))
        peers.append(at_seq(lax.rem(seq + seq_count - o, seq_count)))
    barrier = pltpu.get_barrier_semaphore()
    for peer in peers:
        pl.semaphore_signal(barrier, inc=1, device_id=peer, device_id_type=MESH)

    for source, target in ((wk_ref, wkb), (wv_ref, wvb)):
        padbuf[...] = jnp.zeros_like(padbuf)
        padbuf[0:rows_each, :] = source[...].astype(F32)
        target[zq, zr, x] = padbuf[...].astype(BF16)
    per = slot_count // REACH
    nbf[0:per] = nb_ref[0:per]
    pl.semaphore_wait(barrier, len(peers))

    sems = Sems(send_sem, recv_sem)

    def send(block, devices):
        return [sems.copy(block, block, device) for device in devices]

    stride_devices = [z_peer(QUAD * d) for d in range(1, nq)]
    near_devices = [z_peer(d) for d in z_near]
    x_devices = [x_peer(d) for d in range(1, nx)]
    y_devices = [y_peer(d) for d in range(1, ny)]
    k_stride = send(wkb.at[zq, zr, x], stride_devices)
    v_stride = send(wvb.at[zq, zr, x], stride_devices)
    arriving = {}
    for o in range(1, REACH):
        arriving[o] = sems.copy(
            nb_ref.at[pl.ds(per * o, per)],
            nbf.at[pl.ds(per * o, per)],
            at_seq(lax.rem(seq + seq_count - o, seq_count)),
        )

    first_count = counts_ref[0]
    member = []
    for r in range(slot_count):
        m = jnp.int32(0)
        for i in range(slot_count):
            m = m + jnp.where(owner_ref[i] == r, jnp.where(first_count <= i, 1, 0), 0)
        member.append(m)

    def place():
        col = lax.broadcasted_iota(jnp.int32, (8, padded), 1)
        chunk, e = col // PAD, lax.rem(col, PAD)
        owner = lax.rem(chunk, nx) * nz + chunk // nx
        want = jnp.where(e < rows_each, owner * rows_each + e, -1)[0:1]
        row = lax.broadcasted_iota(jnp.int32, (enc, padded), 0)
        perm[...] = jnp.where(row == want, 1.0, 0.0).astype(BF16)

    def make_bias():
        slot = lax.rem(lax.broadcasted_iota(jnp.int32, (8, keys), 1) // tok, slot_count)
        owned = jnp.zeros((8, keys), jnp.int32)
        for r in range(slot_count):
            owned = jnp.where(slot == r, member[r], owned)
        block = lax.broadcasted_iota(jnp.int32, (queries, keys), 0) // block_len
        bias[...] = jnp.where(block == owned[0:1], 0.0, -jnp.inf)

    def encode(r0, r1):
        n = (r1 - r0) * tok
        states = nbf[r0:r1].reshape(n, enc)
        slot = r0 + lax.broadcasted_iota(jnp.int32, (n, queries), 0) // tok
        owned = jnp.zeros((n, queries), jnp.int32)
        for r in range(r0, r1):
            owned = jnp.where(slot == r, member[r], owned)
        token_block = lax.broadcasted_iota(jnp.int32, (n, queries), 1) // block_len
        ok = token_block == owned
        rows = slice(r0 * tok, r1 * tok)
        parts = [slice(h * HS, (h + 1) * HS) for h in range(enc // HS)]
        scores = [dot(states[:, c], kv_ref[:, c], ((1,), (1,))) for c in parts]
        scores = [jnp.where(ok, s * scale, -jnp.inf) for s in scores]
        tops = [jnp.max(s, axis=1, keepdims=True) for s in scores]
        scores = [jnp.exp(s - t) for s, t in zip(scores, tops)]
        sums = [jnp.sum(p, axis=1, keepdims=True) for p in scores]
        scores = [(p / t).astype(BF16) for p, t in zip(scores, sums)]
        mixed = [
            dot(w, kv_ref[:, enc + h * HS : enc + (h + 1) * HS]) for h, w in enumerate(scores)
        ]
        for c, m in zip(parts, mixed):
            xe[rows, c] = (states[:, c].astype(F32) + m).astype(BF16)
        spread = dot(xe[r0 * tok : r1 * tok, :], perm[...]).astype(BF16)
        xg[y, core, r0:r1] = spread.reshape(r1 - r0, tok, padded)
        mine = xg.at[y, core, pl.ds(r0, r1 - r0)]
        return send(mine, y_devices)

    def cross(r0, r1):
        block = xg.at[:, core, pl.ds(r0, r1 - r0)]
        return send(block, [other_core])

    place()
    cut0, cut1 = per, 3 * per
    share0 = encode(0, cut0)
    make_bias()
    landed(k_stride)
    low, high = pl.ds(0, width // 2), pl.ds(width // 2, width // 2)
    k_near = send(wkb.at[:, zr, x, :, low], near_devices)
    l_x = send(wkb.at[:, zr, x, :, high], x_devices)
    k_x = send(wkb.at[:, zr, x, :, low], x_devices)
    l_near = send(wkb.at[:, zr, x, :, high], near_devices)
    landed(v_stride)
    v_near = send(wvb.at[:, zr, x], near_devices)
    v_x = send(wvb.at[:, zr, x], x_devices)
    landed(arriving[o] for o in (1, 2))
    share1 = encode(1 * per, 3 * per)
    for i, d in enumerate(z_near):
        landed(k_near[i : i + 1])
        k_x += send(wkb.at[:, lax.rem(zr + QUAD - d, QUAD), x, :, low], x_devices)
    landed(arriving[o] for o in (3, 4))
    share2 = encode(3 * per, 5 * per)
    for i, d in enumerate(z_near):
        landed(v_near[i : i + 1])
        v_x += send(wvb.at[:, lax.rem(zr + QUAD - d, QUAD), x], x_devices)
    landed(share0)
    crossing = cross(0, per)
    landed(share1)
    crossing += cross(1 * per, 3 * per)
    for d in range(1, nx):
        landed(l_x[d - 1 : d])
        l_near += send(wkb.at[:, zr, lax.rem(x + nx - d, nx), :, high], near_devices)
    landed(share2)
    crossing += cross(3 * per, 5 * per)
    landed(k_x)
    landed(l_near)
    landed(crossing)

    half_y = ny // 2
    group_rows = keys // 2

    def project(i, weights, target):
        rows = xg[i * half_y : (i + 1) * half_y].reshape(group_rows, padded)
        at = slice(i * group_rows, (i + 1) * group_rows)
        target[at, :] = dot(rows, weights[...].reshape(padded, width)).astype(BF16)

    for i in range(2):
        project(i, wkb, kb)
    landed(v_x)
    for i in range(2):
        project(i, wvb, vb)

    parts = [slice(h * HS, (h + 1) * HS) for h in range(heads)]
    scores = [dot(q_ref[:, c], kb[:, c], ((1,), (1,))) for c in parts]
    scores = [s * scale + bias[...] for s in scores]
    tops = [jnp.max(s, axis=1, keepdims=True) for s in scores]
    weights = [jnp.exp(s - t) for s, t in zip(scores, tops)]
    inverse = [1.0 / jnp.sum(p, axis=1, keepdims=True) for p in weights]
    outs = [dot(p.astype(BF16), vb[:, c]) * t for p, c, t in zip(weights, parts, inverse)]
    weights = [p * t for p, t in zip(weights, inverse)]
    for h, c in enumerate(parts):
        pbuf[h] = weights[h]
        dvb[:, c] = dot(weights[h].astype(BF16), g_ref[:, c], ((0,), (0,))).astype(BF16)
    for h, c in enumerate(parts):
        att_ref[:, c] = outs[h].astype(BF16)
        delta = jnp.sum(g_ref[:, c].astype(F32) * outs[h], axis=1, keepdims=True)
        stats[h] = jnp.broadcast_to(delta, (queries, HS))

    row_tile = padded // nq

    def weight_grad(target, source):
        for i in range(nq):
            lhs = xg[:, :, :, :, i * row_tile : (i + 1) * row_tile].reshape(keys, row_tile)
            part = dot(lhs, source[...], ((0,), (0,)))
            target[i] = part.astype(BF16).reshape(QUAD, nx, PAD, width)

    def exchange_x(block, slots):
        return [
            sems.copy(block(lax.rem(x + d, nx)), slots.at[d - 1], x_peer(d)) for d in range(1, nx)
        ]

    def exchange_near(block, slots):
        half = nq // 2
        copies = []
        for d in (1, -1):
            dst = slots.at[0 if d == 1 else 1]
            copies.append(sems.copy(block(lax.rem(zr + d + QUAD, QUAD)), dst, z_peer(d)))
        for d, first in ((2, 0), (-2, half)):
            src = block(lax.rem(zr + 2, QUAD)).at[pl.ds(first, half)]
            copies.append(sems.copy(src, slots.at[2, pl.ds(first, half)], z_peer(d)))
        return copies

    def exchange_stride(block, slots):
        return [
            sems.copy(block(lax.rem(zq + d, nq)), slots.at[d - 1], z_peer(QUAD * d))
            for d in range(1, nq)
        ]

    def total(own, slots):
        result = own.astype(F32)
        for i in range(slots.shape[0]):
            result = result + slots[i].astype(F32)
        return result

    weight_grad(gvb, dvb)
    gv_x = exchange_x(lambda i: gvb.at[:, :, i], v_slots_x)

    dps = [dot(g_ref[:, c], vb[:, c], ((1,), (1,))) for c in parts]
    dss = [(pbuf[h] * (dp - stats[h][:, 0:1])).astype(BF16) for h, dp in enumerate(dps)]
    for ds, c in zip(dss, parts):
        dkb[:, c] = (dot(ds, q_ref[:, c], ((0,), (0,))) * scale).astype(BF16)
    weight_grad(gkb, dkb)
    gk_near = []
    for d in range(1, nx + 1):
        to = lax.rem(x + d, nx)
        gk_near.append(
            exchange_near(lambda i, to=to: gkb.at[:, i, to], k_slots_near.at[:, :, to])
        )
    for ds, c in zip(dss, parts):
        dq_ref[:, c] = dot(ds, kb[:, c]) * scale
    landed(gv_x)
    v_sum_x[...] = total(gvb[:, :, x], v_slots_x).astype(BF16)
    gv_near = exchange_near(lambda i: v_sum_x.at[:, i], v_slots_near)
    gk_x = []
    for d in range(1, nx + 1):
        to = lax.rem(x + d, nx)
        landed(gk_near[d - 1])
        k_sum_near[:, to] = total(gkb[:, zr, to], k_slots_near.at[:, :, to]).astype(BF16)
        if d < nx:
            gk_x.append(sems.copy(k_sum_near.at[:, to], k_slots_x.at[d - 1], x_peer(d)))
    landed(gv_near)
    v_sum_near[...] = total(v_sum_x[:, zr], v_slots_near).astype(BF16)
    gv_stride = exchange_stride(lambda i: v_sum_near.at[i], v_slots_stride)
    landed(gk_x)
    k_sum_x[...] = total(k_sum_near[:, x], k_slots_x).astype(BF16)
    gk_stride = exchange_stride(lambda i: k_sum_x.at[i], k_slots_stride)
    landed(gv_stride)
    gv_ref[...] = total(v_sum_near[zq], v_slots_stride)[0:rows_each]
    landed(gk_stride)
    gk_ref[...] = total(k_sum_x[zq], k_slots_stride)[0:rows_each]
    sems.finish()


def per_device(sizes, queries, block_kv, nb_states, key_weight, value_weight, counts, owner, grad):
    nx, nz, ny, nc = sizes
    tokens, width = queries.shape
    slot_count, tok, enc = nb_states.shape
    rows_each = key_weight.shape[0]
    heads = width // HS
    padded = nx * nz * PAD
    tp_count = ny * nc
    keys = tp_count * slot_count * tok
    nq = nz // QUAD
    copies = 4 * (nq - 1) + 4 * (nx - 1) + 2 * 3 * nx + (nx - 1) * 3 + 4 * nx + 4
    copies += REACH - 1 + 5 * ny + 4 * (nx - 1) + 3 * nx
    vmem = pl.BlockSpec(memory_space=pltpu.VMEM)
    smem = pl.BlockSpec(memory_space=pltpu.SMEM)
    scratch = [
        pltpu.VMEM((slot_count, tok, enc), BF16),
        pltpu.VMEM((slot_count * tok, enc), BF16),
        pltpu.VMEM((enc, padded), BF16),
        pltpu.VMEM((ny, nc, slot_count, tok, padded), BF16),
        pltpu.VMEM((nq, QUAD, nx, PAD, width), BF16),
        pltpu.VMEM((nq, QUAD, nx, PAD, width), BF16),
        pltpu.VMEM((PAD, width), F32),
        pltpu.VMEM((keys, width), BF16),
        pltpu.VMEM((keys, width), BF16),
        pltpu.VMEM((keys, width), BF16),
        pltpu.VMEM((keys, width), BF16),
        pltpu.VMEM((tokens, keys), F32),
        pltpu.VMEM((heads, tokens, keys), F32),
        pltpu.VMEM((heads, tokens, HS), F32),
        pltpu.VMEM((nq, QUAD, nx, PAD, width), BF16),
        pltpu.VMEM((nq, QUAD, nx, PAD, width), BF16),
        pltpu.VMEM((nx - 1, nq, QUAD, PAD, width), BF16),
        pltpu.VMEM((nq, QUAD, PAD, width), BF16),
        pltpu.VMEM((3, nq, PAD, width), BF16),
        pltpu.VMEM((nq, PAD, width), BF16),
        pltpu.VMEM((nq - 1, PAD, width), BF16),
        pltpu.VMEM((3, nq, nx, PAD, width), BF16),
        pltpu.VMEM((nq, nx, PAD, width), BF16),
        pltpu.VMEM((nx - 1, nq, PAD, width), BF16),
        pltpu.VMEM((nq, PAD, width), BF16),
        pltpu.VMEM((nq - 1, PAD, width), BF16),
        pltpu.SemaphoreType.DMA((copies,)),
        pltpu.SemaphoreType.DMA((copies,)),
    ]
    return pl.pallas_call(
        functools.partial(kernel, sizes),
        out_shape=(
            jax.ShapeDtypeStruct((tokens, width), BF16),
            jax.ShapeDtypeStruct((tokens, width), F32),
            jax.ShapeDtypeStruct((rows_each, width), F32),
            jax.ShapeDtypeStruct((rows_each, width), F32),
        ),
        in_specs=[vmem, vmem, vmem, vmem, vmem, smem, smem, vmem],
        out_specs=(vmem, vmem, vmem, vmem),
        scratch_shapes=scratch,
        compiler_params=pltpu.CompilerParams(
            collective_id=0, has_side_effects=True, vmem_limit_bytes=56 * 1024 * 1024
        ),
        cost_estimate=pl.CostEstimate(
            flops=8 * 10**9, bytes_accessed=2 * 10**6, transcendentals=10**6
        ),
    )(queries, block_kv, nb_states, key_weight, value_weight, counts, owner, grad)


def solution(mesh, sizes=(4, 16, 4, 2)):
    in_specs = (
        P("seq", "tp"),
        P("seq", None),
        P("seq", "tp", None),
        P("seq", "tp"),
        P("seq", "tp"),
        P("seq"),
        P("seq"),
        P("seq", "tp"),
    )
    out_specs = (P("seq", "tp"), P("seq", "tp"), P("seq", "tp"), P("seq", "tp"))
    return jax.shard_map(
        functools.partial(per_device, sizes),
        mesh=mesh,
        in_specs=in_specs,
        out_specs=out_specs,
        check_vma=False,
    )
```
